256 devices in a mesh: row: 16 (over z, y_lo), col: 16 (over y_hi, x, core).
Axes of the slice: x: 4, y: 4 (y_hi: 2, y_lo: 2; y = y_hi * 2 + y_lo), z: 8, core: 2. Of those that a mesh axis runs over, the one named last changes fastest.
Arguments:
- matrix: float32 [2, 8192, 2, 8192], P(None, 'row', None, 'col'), may hold values from -6 to 6
- pivot_rows: int32 [512], replicated, may hold values from 0 to 16383, as said below
- inv_lower: float32 [512, 512], replicated, as said below
- inv_upper: float32 [512, 512], replicated, as said below
Outputs:
- factored: float32 [2, 8192, 2, 8192], P(None, 'row', None, 'col')
The draws below stay inside these ranges and needn't reach their ends.
Inputs may be any that keep to these rules, and one draw needn't show every extreme that they name: Each pivot_rows[i] is either i or a row of 512 or more; no row appears twice. inv_lower is unit lower triangular. inv_upper is upper triangular with a positive diagonal.
All inputs are finite; a program needn't handle non-finite values.
Results may differ from the reference program's by a relative error of at most 0.00008.
Values sent between devices are 32-bit elements; how exact they have to be, the bound alone decides.
No kernel may reach another device: no remote copies, remote signals or barrier semaphores. Data moves between devices by JAX's collectives and lax.ppermute only.
A program may use at most 64 MiB of HBM per device.

```python
import math
import jax
import jax.numpy as jnp
from jax import lax

NB = 512
RT = 2
CT = 2
ROWS = 16384
COLS = 16384
N_ROW = 16
N_COL = 16


def draw_pivot_rows(key, part):
    key = jax.random.fold_in(key, 11)
    key_far, key_stay = jax.random.split(key)
    far_rows = jax.random.permutation(key_far, ROWS - NB - 1)[:NB] + NB
    positions = jnp.arange(NB, dtype=jnp.int32)
    far_rows = jnp.where(positions == NB - 1, ROWS - 1, far_rows)
    stay_flag = jax.random.randint(key_stay, (NB,), 0, 5)
    stay_flag = jnp.where(positions == 0, 0, stay_flag)
    stay_flag = jnp.where(positions == NB - 1, 1, stay_flag)
    return jnp.where(stay_flag == 0, positions, far_rows).astype(jnp.int32)


def draw_inv_lower(key, part):
    key = jax.random.fold_in(key, 12)
    entries = jax.random.normal(key, (NB, NB), jnp.float32)
    strict = jnp.tril(entries * (0.5 / math.sqrt(NB)), -1)
    return (strict + jnp.eye(NB, dtype=jnp.float32)).astype(jnp.float32)


def draw_inv_upper(key, part):
    key = jax.random.fold_in(key, 13)
    key_diag, key_off = jax.random.split(key)
    diagonal = jax.random.uniform(key_diag, (NB,), jnp.float32, 1.0, 3.0) / math.sqrt(NB)
    entries = jax.random.normal(key_off, (NB, NB), jnp.float32)
    strict = jnp.triu(entries * (0.8 / NB), 1)
    return (strict + jnp.diag(diagonal)).astype(jnp.float32)


def block_levels(rng, dims, shards, smallest, top_value):
    factor_of, own = 1.0, jax.random.fold_in(rng, 6)
    for axis_at, shards_of in shards:
        steps = jnp.exp(jax.random.uniform(jax.random.fold_in(own, axis_at), (shards_of,), jnp.float32, smallest / len(shards), top_value / len(shards)))
        factor_of = factor_of * jnp.repeat(steps, dims[axis_at] // shards_of).reshape([-1 if axis == axis_at else 1 for axis in range(len(dims))])
    return factor_of


def normal_values(stream_key, extent, deviation, limit, shards=(), kind=jnp.bfloat16):
    factor_of = block_levels(stream_key, extent, shards, -0.22, 0.18) if shards else 1.0
    drawn = jax.random.normal(stream_key, extent, jnp.float32) * deviation * factor_of
    return jnp.minimum(jnp.maximum(drawn, -limit), limit).astype(kind)


def setup_inputs(seed: int = 0) -> dict:
    key_list = jax.random.split(jax.random.key(seed), 5)
    return {
        "matrix": normal_values(key_list[0], (RT, N_ROW * NB, CT, N_COL * NB), 1.0, 6.0, ((1, 16), (3, 16)), jnp.float32),
        "pivot_rows": draw_pivot_rows(jax.random.fold_in(key_list[4], 71), 0),
        "inv_lower": draw_inv_lower(jax.random.fold_in(key_list[4], 71), 0),
        "inv_upper": draw_inv_upper(jax.random.fold_in(key_list[4], 71), 0),
    }


def reference(matrix, pivot_rows, inv_lower, inv_upper):
    best = lax.Precision.HIGHEST
    whole_matrix = matrix.reshape(ROWS, COLS)
    new_top = whole_matrix[pivot_rows]
    swapped = whole_matrix.at[pivot_rows].set(whole_matrix[:NB])
    swapped = swapped.at[:NB].set(new_top)
    upper_rows = jnp.dot(inv_lower, new_top, precision=best, preferred_element_type=jnp.float32)
    lower_cols = jnp.dot(swapped[NB:, :NB], inv_upper, precision=best, preferred_element_type=jnp.float32)
    trailing = swapped[NB:, NB:] - jnp.dot(lower_cols, upper_rows[:, NB:], precision=best, preferred_element_type=jnp.float32)
    below = jnp.concatenate([lower_cols, trailing], axis=1)
    result = jnp.concatenate([upper_rows, below], axis=0)
    return result.reshape(RT, N_ROW * NB, CT, N_COL * NB)
```

```python
import functools

import jax
import jax.numpy as jnp
from jax import lax
from jax.experimental import pallas as pl
from jax.experimental.pallas import tpu as pltpu
from jax.sharding import PartitionSpec as P

CAP = 48
TILE = 512
LAYERS = 8
MIB = 1024 * 1024


def spread(block, axis, holder):
    block = jnp.where(lax.axis_index(axis) == holder, block, jnp.zeros_like(block))
    return lax.psum(block, axis)


def any_pivots(matrix, pivot_rows, inv_lower, inv_upper):
    best = lax.Precision.HIGHEST
    tiles_down, tile_width, tiles_across, _ = matrix.shape
    row_count = lax.axis_size("row")
    row_index = lax.axis_index("row")
    col_index = lax.axis_index("col")
    local_rows = tiles_down * tile_width
    matrix_here = matrix.reshape(local_rows, tiles_across * tile_width)
    positions = jnp.arange(local_rows, dtype=jnp.int32)
    global_rows = (
        positions // tile_width * row_count + row_index
    ) * tile_width + positions % tile_width
    pivot_tile = pivot_rows // tile_width
    owned = pivot_tile % row_count == row_index
    pivot_local = pivot_tile // row_count * tile_width + pivot_rows % tile_width
    picked = jnp.where(
        owned[:, None], matrix_here[jnp.where(owned, pivot_local, 0)], jnp.float32(0.0)
    )
    former_top = spread(matrix_here[:tile_width], "row", 0)
    matches = (global_rows[:, None] == pivot_rows[None, :]) & (global_rows[:, None] >= tile_width)
    has_source = jnp.any(matches, axis=1)
    source = jnp.sum(
        jnp.where(matches, jnp.arange(tile_width, dtype=jnp.int32)[None, :], 0), axis=1
    )
    swapped = jnp.where(has_source[:, None], former_top[source], matrix_here)
    new_top = lax.psum(picked, "row")
    upper_rows = jnp.dot(inv_lower, new_top, precision=best, preferred_element_type=jnp.float32)
    panel_rows = swapped[:, :tile_width]
    solved_panel = jnp.dot(
        panel_rows, inv_upper, precision=best, preferred_element_type=jnp.float32
    )
    lower_cols = spread(solved_panel, "col", 0)
    updated = swapped - jnp.dot(
        lower_cols, upper_rows, precision=best, preferred_element_type=jnp.float32
    )
    leading = jnp.where(col_index == 0, lower_cols, updated[:, :tile_width])
    result = jnp.concatenate([leading, updated[:, tile_width:]], axis=1)
    first_rows = jnp.where(row_index == 0, upper_rows, result[:tile_width])
    result = jnp.concatenate([first_rows, result[tile_width:]], axis=0)
    return result.reshape(tiles_down, tile_width, tiles_across, tile_width)


def as_rows(matrix):
    return matrix.reshape(1024, 2, 4, 128).transpose(0, 2, 1, 3).reshape(1024, 8, 128)


def as_matrix(rows):
    return rows.reshape(1024, 4, 2, 128).transpose(0, 2, 1, 3).reshape(2, 512, 2, 512)


def split(value):
    high = value.astype(jnp.bfloat16)
    low = (value - high.astype(jnp.float32)).astype(jnp.bfloat16)
    return high, low


def dot3(a_high, a_low, b_high, b_low):
    dot = functools.partial(jnp.dot, preferred_element_type=jnp.float32)
    return dot(a_high, b_high) + (dot(a_high, b_low) + dot(a_low, b_high))


def solve_kernel(rows_ref, panel_ref, sent_ref, inv_ref, out_ref, swapped):
    swapped[...] = panel_ref[...]

    @pl.loop(0, rows_ref[0])
    def _(k):
        swapped[pl.ds(rows_ref[8 + k], 1), :] = sent_ref[pl.ds(k, 1), :]

    inv_high, inv_low = split(inv_ref[...])

    @pl.loop(0, 4)
    def _(b):
        at = pl.ds(pl.multiple_of(b * 256, 256), 256)
        high, low = split(swapped[at, :])
        out_ref[at, :] = dot3(high, low, inv_high, inv_low)


def solve(rows, panel, sent, inv_upper):
    vmem = pl.BlockSpec(memory_space=pltpu.VMEM)
    return pl.pallas_call(
        solve_kernel,
        out_shape=jax.ShapeDtypeStruct((1024, 512), jnp.float32),
        in_specs=[pl.BlockSpec(memory_space=pltpu.SMEM), vmem, vmem, vmem],
        out_specs=vmem,
        scratch_shapes=[pltpu.VMEM((1024, 512), jnp.float32)],
        compiler_params=pltpu.CompilerParams(vmem_limit_bytes=24 * MIB),
        cost_estimate=pl.CostEstimate(flops=3 * 2 * 1024 * 512 * 512, bytes_accessed=6 * MIB, transcendentals=0),
        name="solve",
    )(rows, panel, sent, inv_upper)


def upper_kernel(top_ref, pivot_ref, w_ref, u_ref, high_ref, low_ref, g_high, g_low):
    for sub in range(8):
        at = slice(128 * sub, 128 * sub + 128)
        high, low = split(top_ref[pl.ds(sub, 512, stride=8), :])
        g_high[:512, at], g_low[:512, at] = high, low
        high, low = split(pivot_ref[pl.ds(sub, 16 * CAP, stride=8), :])
        g_high[512:, at], g_low[512:, at] = high, low
    w_high, w_low = split(w_ref[...])
    for n in range(4):
        at = slice(256 * n, 256 * n + 256)
        u = dot3(w_high, w_low, g_high[:, at], g_low[:, at])
        high, low = split(u)
        high_ref[:, at], low_ref[:, at] = high, low
        u_ref[pl.ds(2 * n, 512, stride=8), :] = u[:, :128]
        u_ref[pl.ds(2 * n + 1, 512, stride=8), :] = u[:, 128:]


def upper(top, pivots, weights):
    depth = 512 + 16 * CAP
    vmem = pl.BlockSpec(memory_space=pltpu.VMEM)
    half = jax.ShapeDtypeStruct((512, 1024), jnp.bfloat16)
    return pl.pallas_call(
        upper_kernel,
        out_shape=[jax.ShapeDtypeStruct((4096, 128), jnp.float32), half, half],
        in_specs=[vmem] * 3,
        out_specs=[vmem] * 3,
        scratch_shapes=[pltpu.VMEM((depth, 1024), jnp.bfloat16)] * 2,
        compiler_params=pltpu.CompilerParams(vmem_limit_bytes=40 * MIB),
        cost_estimate=pl.CostEstimate(flops=3 * 2 * 512 * depth * 1024, bytes_accessed=12 * MIB, transcendentals=0),
        name="upper",
    )(top, pivots, weights)


def trailing_kernel(rows_ref, x_ref, lower_ref, high_ref, low_ref, top_ref, u_ref, out_ref):
    block = pl.program_id(0)
    out_ref[...] = x_ref[...]

    @pl.loop(0, rows_ref[0])
    def _(k):
        row = rows_ref[8 + k] - block * 256

        @pl.when((row >= 0) & (row < 256))
        def _():
            to = pl.ds(pl.multiple_of(row * 8, 8), 8)
            out_ref[to, :] = top_ref[pl.ds(pl.multiple_of(rows_ref[8 + CAP + k] * 8, 8), 8), :]

    l_high, l_low = split(lower_ref[...])
    for n in range(4):
        at = slice(256 * n, 256 * n + 256)
        product = dot3(l_high, l_low, high_ref[:, at], low_ref[:, at])
        for part in range(2):
            to = pl.ds(2 * n + part, 256, stride=8)
            out_ref[to, :] = out_ref[to, :] - product[:, 128 * part : 128 * part + 128]

    @pl.when(rows_ref[2] == 0)
    def _():
        for l in range(4):
            out_ref[pl.ds(2 * l, 256, stride=8), :] = lower_ref[:, 128 * l : 128 * l + 128]

    @pl.when((rows_ref[1] == 0) & (block < 2))
    def _():
        out_ref[...] = u_ref[pl.ds(pl.multiple_of(lax.rem(block, 2) * 2048, 2048), 2048), :]


def trailing(rows, x, lower, high, low, top, u):
    whole = lambda *shape: pl.BlockSpec(shape, lambda i, *_: (0, 0))
    return pl.pallas_call(
        trailing_kernel,
        out_shape=jax.ShapeDtypeStruct((8192, 128), jnp.float32),
        grid_spec=pltpu.PrefetchScalarGridSpec(
            num_scalar_prefetch=1,
            grid=(4,),
            in_specs=[
                pl.BlockSpec((2048, 128), lambda i, *_: (i, 0)),
                pl.BlockSpec((256, 512), lambda i, *_: (i, 0)),
                whole(512, 1024),
                whole(512, 1024),
                whole(4096, 128),
                whole(4096, 128),
            ],
            out_specs=pl.BlockSpec((2048, 128), lambda i, *_: (i, 0)),
        ),
        compiler_params=pltpu.CompilerParams(vmem_limit_bytes=40 * MIB),
        cost_estimate=pl.CostEstimate(flops=3 * 2 * 1024 * 512 * 1024, bytes_accessed=16 * MIB, transcendentals=0),
        name="trailing",
    )(rows, x, lower, high, low, top, u)


def z_shift(value, by):
    return lax.ppermute(value, "row", [(i, (i // 2 + by) % LAYERS * 2 + i % 2) for i in range(16)])


def x_shift(value, by):
    return lax.ppermute(value, "col", [(i, i // 8 * 8 + (i // 2 + by) % 4 * 2 + i % 2) for i in range(16)])


def swap(value, axis):
    return lax.ppermute(value, axis, [(i, i ^ 1) for i in range(16)])


def ring(piece):
    up = down = piece
    pieces = [piece]
    for _ in range(3):
        up, down = z_shift(up, 1), z_shift(down, -1)
        pieces += [up, down]
    half = piece.shape[0] // 2
    pieces += [z_shift(up[:half], 1), z_shift(down[half:], -1)]
    return jnp.concatenate(pieces)


def broadcast_panel(lower, col):
    core, x, h = col % 2, col // 2 % 4, col // 8
    second = lax.ppermute(lower[512:], "col", [(0, 1)])
    half = jnp.where(core == 0, lower[:512], second)
    mine = half[:128]
    for to in (1, 3, 2):
        got = lax.ppermute(half[128 * to : 128 * to + 128], "col", [(0, 2 * to), (1, 2 * to + 1)])
        mine = jnp.where(x == to, got, mine)
    got = lax.ppermute(mine, "col", [(i, i + 8) for i in range(8)])
    mine = jnp.where(h == 0, mine, got)
    up, down = x_shift(mine, 1), x_shift(mine, -1)
    opposite = jnp.concatenate([x_shift(up[:64], 1), x_shift(down[64:], -1)])
    pieces = [mine, up, opposite, down]
    order = [
        lax.select_n(x, pieces[-i % 4], pieces[(1 - i) % 4], pieces[(2 - i) % 4], pieces[(3 - i) % 4])
        for i in range(4)
    ]
    half = jnp.concatenate(order)
    other = swap(half, "col")
    return jnp.concatenate([jnp.where(core == 0, half, other), jnp.where(core == 0, other, half)])


def few_pivots(matrix, pivot_rows, inv_lower, inv_upper, owner, rank):
    best = lax.Precision.HIGHEST
    row, col = lax.axis_index("row"), lax.axis_index("col")
    z, y = row // 2, row % 2
    x3 = as_rows(matrix)
    top = x3[:TILE]
    panel = matrix[:, :, 0, :].reshape(1024, TILE)
    index = jnp.arange(TILE, dtype=jnp.int32)
    slots = jnp.arange(CAP, dtype=jnp.int32)
    moved = owner >= 0
    here = pivot_rows // TILE // 16 * TILE + pivot_rows % TILE

    mine = (owner[:, None] == row) & (rank[:, None] == slots[None, :])
    at_rows = jnp.sum(jnp.where(mine, here[:, None], 0), axis=0)
    from_top = jnp.sum(jnp.where(mine, index[:, None], 0), axis=0)
    count = jnp.sum((owner == row).astype(jnp.int32))
    place = jnp.array([0, 2, 4, 6, 7, 5, 3, 1], jnp.int32)
    top_place = place[(from_top // 64 - z) % LAYERS] * 64 + from_top % 64
    head = jnp.concatenate([count[None], row[None], col[None], jnp.zeros(5, jnp.int32)])
    rows = jnp.concatenate([head.astype(jnp.int32), at_rows, top_place])

    all_owner = jnp.arange(16 * CAP, dtype=jnp.int32) // CAP
    all_rank = jnp.arange(16 * CAP, dtype=jnp.int32) % CAP
    chosen = (owner[None, :] == all_owner[:, None]) & (rank[None, :] == all_rank[:, None])
    table = jnp.dot(chosen.astype(jnp.float32), panel[:TILE], precision=best, preferred_element_type=jnp.float32)
    sent = jnp.where(row == 0, table[: 2 * CAP], 0.0)
    for to in range(1, LAYERS):
        sent = sent + lax.ppermute(
            table[2 * CAP * to : 2 * CAP * (to + 1)], ("row", "col"), [(0, 2 * to * 16)]
        )
    sent_up = lax.ppermute(sent[CAP:], ("row", "col"), [(2 * to * 16, (2 * to + 1) * 16) for to in range(LAYERS)])
    sent = jnp.where(y == 0, sent[:CAP], sent_up)
    lower = solve(rows, panel, sent, inv_upper)
    lower = broadcast_panel(lower, col)

    picked = x3[at_rows]
    pivots = ring(jnp.concatenate([picked, swap(picked, "row")]))

    piece = jnp.where(z == 0, top[:64], 0.0)
    for to in range(1, LAYERS):
        piece = piece + lax.ppermute(top[64 * to : 64 * to + 64], "row", [(0, 2 * to)])
    other = lax.ppermute(piece, "row", [(2 * i, 2 * i + 1) for i in range(LAYERS)])
    tops = ring(jnp.where(y == 0, piece, other))

    layer = jnp.array([0, -1, 1, -2, 2, -3, 3, 4], jnp.int32)
    layers = (z + layer) % LAYERS
    top_rows = (layers[:, None] * 64 + jnp.arange(64, dtype=jnp.int32)[None, :]).reshape(-1)
    keep = (index[:, None] == top_rows[None, :]) & ~moved[:, None]
    slot_owner = (layers[:, None] * 2 + (y ^ jnp.arange(2, dtype=jnp.int32))[None, :]).reshape(-1)
    slot_owner = jnp.repeat(slot_owner, CAP)
    take = (owner[:, None] == slot_owner[None, :]) & (rank[:, None] == all_rank[None, :])
    choice = jnp.concatenate([keep, take], axis=1).astype(jnp.float32)
    weights = jnp.dot(inv_lower, choice, precision=best, preferred_element_type=jnp.float32)

    tops = tops.reshape(4096, 128)
    u, high, low = upper(tops, pivots.reshape(16 * CAP * 8, 128), weights)
    out = trailing(rows, x3.reshape(8192, 128), lower, high, low, tops, u)
    return as_matrix(out.reshape(1024, 8, 128))


def local(matrix, pivot_rows, inv_lower, inv_upper):
    moved = pivot_rows >= TILE
    owner = jnp.where(moved, pivot_rows // TILE % 16, -1)
    index = jnp.arange(TILE, dtype=jnp.int32)
    before = (owner[:, None] == owner[None, :]) & (index[None, :] < index[:, None])
    rank = jnp.sum(before.astype(jnp.int32), axis=1)
    few = jnp.max(jnp.where(moved, rank, 0)) < CAP
    return lax.cond(
        few,
        few_pivots,
        lambda m, p, l, u, *_: any_pivots(m, p, l, u),
        matrix, pivot_rows, inv_lower, inv_upper, owner, rank,
    )


def solution(mesh):
    return jax.shard_map(
        local,
        mesh=mesh,
        in_specs=(P(None, "row", None, "col"), P(), P(), P()),
        out_specs=P(None, "row", None, "col"),
        check_vma=False,
    )
```

```python
import functools

import jax
import jax.numpy as jnp
from jax import lax
from jax.experimental import pallas as pl
from jax.experimental.pallas import tpu as pltpu
from jax.sharding import PartitionSpec as P

CAP = 48
TILE = 512
LAYERS = 8
MIB = 1024 * 1024
VMEM = 60 * MIB
FAR, NEAR = (4, 3, 5, 2), (6, 1, 7, 0)


def spread(block, axis, holder):
    block = jnp.where(lax.axis_index(axis) == holder, block, jnp.zeros_like(block))
    return lax.psum(block, axis)


def any_pivots(matrix, pivot_rows, inv_lower, inv_upper):
    best = lax.Precision.HIGHEST
    tiles_down, tile_width, tiles_across, _ = matrix.shape
    row_count = lax.axis_size("row")
    row_index = lax.axis_index("row")
    col_index = lax.axis_index("col")
    local_rows = tiles_down * tile_width
    matrix_here = matrix.reshape(local_rows, tiles_across * tile_width)
    positions = jnp.arange(local_rows, dtype=jnp.int32)
    global_rows = (
        positions // tile_width * row_count + row_index
    ) * tile_width + positions % tile_width
    pivot_tile = pivot_rows // tile_width
    owned = pivot_tile % row_count == row_index
    pivot_local = pivot_tile // row_count * tile_width + pivot_rows % tile_width
    picked = jnp.where(
        owned[:, None], matrix_here[jnp.where(owned, pivot_local, 0)], jnp.float32(0.0)
    )
    former_top = spread(matrix_here[:tile_width], "row", 0)
    matches = (global_rows[:, None] == pivot_rows[None, :]) & (global_rows[:, None] >= tile_width)
    has_source = jnp.any(matches, axis=1)
    source = jnp.sum(
        jnp.where(matches, jnp.arange(tile_width, dtype=jnp.int32)[None, :], 0), axis=1
    )
    swapped = jnp.where(has_source[:, None], former_top[source], matrix_here)
    new_top = lax.psum(picked, "row")
    upper_rows = jnp.dot(inv_lower, new_top, precision=best, preferred_element_type=jnp.float32)
    panel_rows = swapped[:, :tile_width]
    solved_panel = jnp.dot(
        panel_rows, inv_upper, precision=best, preferred_element_type=jnp.float32
    )
    lower_cols = spread(solved_panel, "col", 0)
    updated = swapped - jnp.dot(
        lower_cols, upper_rows, precision=best, preferred_element_type=jnp.float32
    )
    leading = jnp.where(col_index == 0, lower_cols, updated[:, :tile_width])
    result = jnp.concatenate([leading, updated[:, tile_width:]], axis=1)
    first_rows = jnp.where(row_index == 0, upper_rows, result[:tile_width])
    result = jnp.concatenate([first_rows, result[tile_width:]], axis=0)
    return result.reshape(tiles_down, tile_width, tiles_across, tile_width)


def as_rows(matrix):
    return matrix.reshape(1024, 2, 4, 128).transpose(0, 2, 1, 3).reshape(1024, 8, 128)


def as_matrix(rows):
    return rows.reshape(1024, 4, 2, 128).transpose(0, 2, 1, 3).reshape(2, 512, 2, 512)


def split(value):
    high = value.astype(jnp.bfloat16)
    low = (value - high.astype(jnp.float32)).astype(jnp.bfloat16)
    return high, low


def dot3(a_high, a_low, b_high, b_low):
    dot = functools.partial(jnp.dot, preferred_element_type=jnp.float32)
    return dot(a_high, b_high) + (dot(a_high, b_low) + dot(a_low, b_high))


def whole(memory, count):
    return [pl.BlockSpec(memory_space=memory)] * count


def prepare_kernel(rows_ref, key_ref, x_ref, first_ref, second_ref, picked_ref, *rest):
    outs, (x_here, load) = rest[: LAYERS + 2], rest[LAYERS + 2 :]
    loads = [
        pltpu.make_async_copy(x_ref.at[pl.ds(2048 * b, 2048)], x_here.at[pl.ds(2048 * b, 2048)], load.at[b])
        for b in range(4)
    ]
    for copy in loads:
        copy.start()
    places = [(outs[k // 2], 0) for k in range(16)]
    for group, out in zip((FAR, NEAR), outs[LAYERS:]):
        for at, k in enumerate(group):
            places[2 * k + 1] = (out, 320 * at)
    for b in range(4):
        loads[b].wait()
        out_ref = (first_ref, second_ref)[b // 2]
        for l in range(4):
            out_ref[256 * (b % 2) : 256 * (b % 2) + 256, 128 * l : 128 * l + 128] = x_here[
                pl.ds(2048 * b + 2 * l, 256, stride=8), :
            ]
        for k, (out, at) in enumerate(places):
            if k // 8 == b:
                out[at : at + 256, :] = x_here[256 * k : 256 * (k + 1), :]
                out[at + 256 : at + 320, :] = jnp.zeros((64, 128), jnp.float32)

    @pl.loop(0, CAP)
    def _(k):
        picked_ref[pl.ds(pl.multiple_of(k * 8, 8), 8), :] = x_here[
            pl.ds(pl.multiple_of(rows_ref[8 + k] * 8, 8), 8), :
        ]

    @pl.when(rows_ref[2] == 0)
    def _():
        tile = first_ref[...]
        high = tile.astype(jnp.bfloat16)
        rest_of = tile - high.astype(jnp.float32)
        middle = rest_of.astype(jnp.bfloat16)
        low = (rest_of - middle.astype(jnp.float32)).astype(jnp.bfloat16)
        for part in range(4):
            slot = lax.broadcasted_iota(jnp.int32, (4 * CAP, TILE), 0) + 4 * CAP * part
            choose = jnp.where(slot == key_ref[...], 1.0, 0.0).astype(jnp.bfloat16)
            dot = functools.partial(jnp.dot, choose, preferred_element_type=jnp.float32)
            table = dot(high) + (dot(middle) + dot(low))
            for k in range(4):
                out, at = places[4 * part + k]
                for l in range(4):
                    cols = slice(128 * l, 128 * l + 128)
                    out[pl.ds(at + 2 * l, 40, stride=8), :] = table[CAP * k : CAP * k + 40, cols]
                    out[pl.ds(at + 256 + 2 * l + 1, 8, stride=8), :] = table[CAP * k + 40 : CAP * k + 48, cols]


def prepare(rows, key, x):
    half = jax.ShapeDtypeStruct((512, 512), jnp.float32)
    picked = jax.ShapeDtypeStruct((CAP * 8, 128), jnp.float32)
    piece = jax.ShapeDtypeStruct((320, 128), jnp.float32)
    group = jax.ShapeDtypeStruct((1280, 128), jnp.float32)
    return pl.pallas_call(
        prepare_kernel,
        out_shape=[half, half, picked] + [piece] * LAYERS + [group] * 2,
        in_specs=whole(pltpu.SMEM, 1) + whole(pltpu.VMEM, 1) + whole(pl.ANY, 1),
        out_specs=whole(pltpu.VMEM, LAYERS + 5),
        scratch_shapes=[pltpu.VMEM((8192, 128), jnp.float32), pltpu.SemaphoreType.DMA((4,))],
        compiler_params=pltpu.CompilerParams(vmem_limit_bytes=VMEM),
        cost_estimate=pl.CostEstimate(flops=2 * 10**9, bytes_accessed=10 * MIB, transcendentals=0),
        name="prepare",
    )(rows, key, x)


def spread_rows(ref, g_high, g_low):
    count = ref.shape[0] // 8
    for sub in range(8):
        high, low = split(ref[pl.ds(sub, count, stride=8), :])
        g_high[:, 128 * sub : 128 * sub + 128] = high
        g_low[:, 128 * sub : 128 * sub + 128] = low


def early_kernel(
    rows_ref, half_ref, other_ref, inv_ref, pivots_ref, take_ref, keep_ref, x_ref,
    m_ref, lw_high, lw_low, part_high, part_low, panel, l_high, l_low, g_high, g_low, u_ref, load,
):
    copy = pltpu.make_async_copy(x_ref, m_ref, load)
    copy.start()
    core, x = rows_ref[2] % 2, rows_ref[2] // 2 % 4
    for ref, tile in ((half_ref, core), (other_ref, 1 - core)):
        for at, size, ahead, skip in ((0, 128, 0, 0), (128, 128, 3, 0), (256, 128, 1, 0), (384, 64, 2, 0), (448, 64, 2, 64)):
            to = tile * 512 + lax.rem(x + ahead, 4) * 128 + skip
            panel[pl.ds(pl.multiple_of(to, 64), size), :] = ref[at : at + size, :]

    spread_rows(pivots_ref, g_high, g_low)
    take_high, take_low = split(take_ref[...])
    for n in range(4):
        at = slice(256 * n, 256 * n + 256)
        u_ref[:, at] = dot3(take_high, take_low, g_high[:, at], g_low[:, at])
    for n in range(4):
        at = slice(256 * n, 256 * n + 256)
        part_high[:, at], part_low[:, at] = split(u_ref[:, at])

    inv_high, inv_low = split(inv_ref[...])
    keep_high, keep_low = split(keep_ref[...])

    @pl.loop(0, 4)
    def _(b):
        at = pl.ds(pl.multiple_of(b * 256, 256), 256)
        high, low = split(panel[at, :])
        high, low = split(dot3(high, low, inv_high, inv_low))
        l_high[at, :], l_low[at, :] = high, low
        lw_high[at, :], lw_low[at, :] = split(dot3(high, low, keep_high, keep_low))

    copy.wait()

    @pl.loop(0, 4)
    def _(b):
        at = pl.ds(pl.multiple_of(b * 256, 256), 256)
        high, low = l_high[at, :], l_low[at, :]
        for n in range(4):
            cols = slice(256 * n, 256 * n + 256)
            product = dot3(high, low, part_high[:, cols], part_low[:, cols])
            for part in range(2):
                to = pl.ds(pl.multiple_of(b * 2048, 2048) + 2 * n + part, 256, stride=8)
                m_ref[to, :] = m_ref[to, :] - product[:, 128 * part : 128 * part + 128]

    @pl.when(rows_ref[2] == 0)
    def _():
        for l in range(4):
            cols = slice(128 * l, 128 * l + 128)
            m_ref[pl.ds(2 * l, 1024, stride=8), :] = l_high[:, cols].astype(jnp.float32) + l_low[:, cols].astype(jnp.float32)

    @pl.when(rows_ref[1] == 0)
    def _():
        for sub in range(8):
            m_ref[pl.ds(sub, 512, stride=8), :] = u_ref[:, 128 * sub : 128 * sub + 128]
        lw_high[:512, :], lw_low[:512, :] = -keep_high, -keep_low


def early(rows, half, other, inv_upper, pivots, take, keep, x):
    part = jax.ShapeDtypeStruct((1024, 512), jnp.bfloat16)
    upper = jax.ShapeDtypeStruct((512, 1024), jnp.bfloat16)
    half_scratch = pltpu.VMEM((1024, 512), jnp.bfloat16)
    return pl.pallas_call(
        early_kernel,
        out_shape=[jax.ShapeDtypeStruct((8192, 128), jnp.float32), part, part, upper, upper],
        in_specs=whole(pltpu.SMEM, 1) + whole(pltpu.VMEM, 6) + whole(pl.ANY, 1),
        out_specs=whole(pltpu.VMEM, 5),
        scratch_shapes=[
            pltpu.VMEM((1024, 512), jnp.float32),
            half_scratch,
            half_scratch,
            pltpu.VMEM((16 * CAP, 1024), jnp.bfloat16),
            pltpu.VMEM((16 * CAP, 1024), jnp.bfloat16),
            pltpu.VMEM((512, 1024), jnp.float32),
            pltpu.SemaphoreType.DMA(()),
        ],
        compiler_params=pltpu.CompilerParams(vmem_limit_bytes=VMEM),
        cost_estimate=pl.CostEstimate(flops=9 * 10**9, bytes_accessed=24 * MIB, transcendentals=0),
        name="early",
    )(rows, half, other, inv_upper, pivots, take, keep, x)


def patch_kernel(rows_ref, sent_ref, inv_ref, keep_ref, part_high, part_low, out_ref, lw_high, lw_low):
    high, low = split(dot3(*split(sent_ref[...]), *split(inv_ref[...])))
    lw_high[...], lw_low[...] = split(dot3(high, low, *split(keep_ref[...])))
    product = dot3(high, low, part_high[...], part_low[...])
    for sub in range(8):
        out_ref[pl.ds(sub, CAP, stride=8), :] = -product[:, 128 * sub : 128 * sub + 128]

    @pl.when(rows_ref[2] == 0)
    def _():
        lower = high.astype(jnp.float32) + low.astype(jnp.float32)
        for l in range(4):
            out_ref[pl.ds(2 * l, CAP, stride=8), :] = lower[:, 128 * l : 128 * l + 128]


def patch(rows, sent, inv_upper, keep, part_high, part_low):
    lw = jax.ShapeDtypeStruct((CAP, 512), jnp.bfloat16)
    return pl.pallas_call(
        patch_kernel,
        out_shape=[jax.ShapeDtypeStruct((CAP * 8, 128), jnp.float32), lw, lw],
        in_specs=whole(pltpu.SMEM, 1) + whole(pltpu.VMEM, 5),
        out_specs=whole(pltpu.VMEM, 3),
        compiler_params=pltpu.CompilerParams(vmem_limit_bytes=VMEM),
        cost_estimate=pl.CostEstimate(flops=10**9, bytes_accessed=4 * MIB, transcendentals=0),
        name="patch",
    )(rows, sent, inv_upper, keep, part_high, part_low)


def late_kernel(
    rows_ref, m_ref, lw_high, lw_low, new_ref, new_high, new_low, x_all, top_all, out_ref, top, g_high, g_low, new, load
):
    block = pl.program_id(0)
    parity = lax.rem(lax.broadcasted_iota(jnp.int32, (8, 128), 0), 2)

    @pl.when(block == 0)
    def _():
        copies = [pltpu.make_async_copy(ref.at[pl.ds(0, 4096)], top, load) for ref in (x_all, top_all)]
        for owned, copy in zip((rows_ref[1] == 0, rows_ref[1] != 0), copies):
            pl.when(owned)(copy.start)
        for owned, copy in zip((rows_ref[1] == 0, rows_ref[1] != 0), copies):
            pl.when(owned)(copy.wait)
        spread_rows(top, g_high, g_low)
        product = dot3(new_high[...], new_low[...], g_high[...], g_low[...])
        for sub in range(8):
            new[pl.ds(sub, CAP, stride=8), :] = product[:, 128 * sub : 128 * sub + 128]

    high, low = lw_high[...], lw_low[...]
    solved = (rows_ref[2] == 0) & ((rows_ref[1] != 0) | (block >= 2))
    for n in range(4):
        cols = slice(256 * n, 256 * n + 256)
        product = dot3(high, low, g_high[:, cols], g_low[:, cols])
        for part in range(2):
            at = pl.ds(2 * n + part, 256, stride=8)
            value = product[:, 128 * part : 128 * part + 128]
            if part == 0:
                value = jnp.where(solved, 0.0, value)
            out_ref[at, :] = m_ref[at, :] - value

    @pl.loop(0, rows_ref[0])
    def _(k):
        row = rows_ref[8 + k] - block * 256

        @pl.when((row >= 0) & (row < 256))
        def _():
            at = pl.ds(pl.multiple_of(k * 8, 8), 8)
            change = top[pl.ds(pl.multiple_of(rows_ref[8 + CAP + k] * 8, 8), 8), :] - new[at, :]
            change = jnp.where((parity == 1) | (rows_ref[2] != 0), change, 0.0)
            out_ref[pl.ds(pl.multiple_of(row * 8, 8), 8), :] = new_ref[at, :] + change


def late(rows, m, lw_high, lw_low, new, new_high, new_low, x, top):
    block = lambda *shape: pl.BlockSpec(shape, lambda i, *_: (i, 0))
    return pl.pallas_call(
        late_kernel,
        out_shape=jax.ShapeDtypeStruct((8192, 128), jnp.float32),
        grid_spec=pltpu.PrefetchScalarGridSpec(
            num_scalar_prefetch=1,
            grid=(4,),
            in_specs=[block(2048, 128), block(256, 512), block(256, 512)]
            + whole(pltpu.VMEM, 3)
            + whole(pl.ANY, 2),
            out_specs=block(2048, 128),
            scratch_shapes=[pltpu.VMEM((4096, 128), jnp.float32)]
            + [pltpu.VMEM((512, 1024), jnp.bfloat16)] * 2
            + [pltpu.VMEM((CAP * 8, 128), jnp.float32), pltpu.SemaphoreType.DMA(())],
        ),
        compiler_params=pltpu.CompilerParams(vmem_limit_bytes=VMEM),
        cost_estimate=pl.CostEstimate(flops=3 * 2 * 1024 * 512 * 1024, bytes_accessed=12 * MIB, transcendentals=0),
        name="late",
    )(rows, m, lw_high, lw_low, new, new_high, new_low, x, top)


def x_shift(value, by):
    return lax.ppermute(value, "col", [(i, i // 8 * 8 + (i // 2 + by) % 4 * 2 + i % 2) for i in range(16)])


def swap(value, axis):
    return lax.ppermute(value, axis, [(i, i ^ 1) for i in range(16)])


def gather_layers(piece):
    groups = [[2 * i + j for i in range(LAYERS)] for j in range(2)]
    return lax.all_gather(piece, "row", axis_index_groups=groups, axis=0, tiled=True)


def across(value, col):
    value = jnp.where(col == 0, value, 0.0)
    value = value + lax.ppermute(value, "col", [(0, 1)])
    got = [lax.ppermute(value, "col", [(0, 2 * to), (1, 2 * to + 1)]) for to in (1, 3, 2)]
    value = value + got[0] + got[1] + got[2]
    return value + lax.ppermute(value, "col", [(i, i + 8) for i in range(8)])


def scatter_panel(first, second, col, before, between):
    core, x = col % 2, col // 2 % 4
    half = jnp.where(core == 0, first, lax.ppermute(second, "col", [(0, 1)])) + 0.0 * before[0, 0]
    mine = jnp.where(x == 0, half[:128], 0.0 * between[0, 0])
    got = [
        lax.ppermute(half[128 * to : 128 * to + 128], "col", [(0, 2 * to), (1, 2 * to + 1)])
        for to in (1, 3, 2)
    ]
    return jnp.where(col < 8, mine + got[0] + got[1] + got[2], 0.0)


def gather_panel(mine):
    mine = mine + lax.ppermute(mine, "col", [(i, i + 8) for i in range(8)])
    up, down = x_shift(mine, 1), x_shift(mine, -1)
    last = [x_shift(up[:64], 1), x_shift(down[64:], -1)]
    return jnp.concatenate([mine, up, down] + last), last[0][0, 0] + last[1][0, 0]


def few_pivots(matrix, pivot_rows, inv_lower, inv_upper, owner, rank):
    best = lax.Precision.HIGHEST
    row, col = lax.axis_index("row"), lax.axis_index("col")
    z, y = row // 2, row % 2
    x2 = as_rows(matrix).reshape(8192, 128)

    index = jnp.arange(TILE, dtype=jnp.int32)
    slots = jnp.arange(CAP, dtype=jnp.int32)
    here = pivot_rows // TILE // 16 * TILE + pivot_rows % TILE
    mine = (owner[:, None] == row) & (rank[:, None] == slots[None, :])
    at_rows = jnp.sum(jnp.where(mine, here[:, None], 0), axis=0)
    from_top = jnp.sum(jnp.where(mine, index[:, None], 0), axis=0)
    count = jnp.minimum(jnp.sum((owner == row).astype(jnp.int32)), CAP)
    head = jnp.stack([count, row, col] + [jnp.int32(0)] * 5).astype(jnp.int32)
    rows = jnp.concatenate([head, at_rows, from_top])
    key = jnp.where(owner < 0, -1, owner * CAP + jnp.minimum(rank, CAP - 1))[None]
    first, second, picked, *packed = prepare(rows, key, x2)

    paired = swap(picked, "row")
    paired = jnp.concatenate([jnp.where(y == 0, picked, paired), jnp.where(y == 0, paired, picked)])
    pivots = gather_layers(paired)

    handed = [lax.ppermute(value, "row", [(0, 1)]) for value in packed[LAYERS:]]
    odd = {}
    for group, value in zip((FAR, NEAR), handed):
        odd.update({k: value[320 * at : 320 * at + 320] for at, k in enumerate(group)})

    half, token = gather_panel(scatter_panel(first, second, col, *handed))
    other_half = swap(half, "col")

    pieces = [jnp.where(row == 0, packed[k], odd[k]) for k in range(LAYERS)]
    piece = jnp.where(z == 0, pieces[0], 0.0 * token)
    for to in FAR + NEAR[:-1]:
        piece = piece + lax.ppermute(pieces[to], "row", [(0, 2 * to), (1, 2 * to + 1)])
    other = swap(piece[:256], "row")
    tops = gather_layers(
        jnp.concatenate([jnp.where(y == 0, piece[:256], other), jnp.where(y == 0, other, piece[:256])])
    )

    extra = piece.reshape(40, 4, 2, 128)
    sent = jnp.concatenate([extra[:, :, 0], extra[32:, :, 1]]).reshape(CAP, TILE)
    sent = across(sent, col)

    take = (key[0][:, None] == jnp.arange(16 * CAP, dtype=jnp.int32)[None, :]) & (rank < CAP)[:, None]
    taken = jnp.dot(inv_lower, take.astype(jnp.float32), precision=best, preferred_element_type=jnp.float32)
    kept = jnp.where((owner < 0)[None, :], inv_lower, 0.0)
    m, lw_high, lw_low, part_high, part_low = early(rows, half, other_half, inv_upper, pivots, taken, kept, x2)
    new, new_high, new_low = patch(rows, sent, inv_upper, kept, part_high, part_low)
    out = late(rows, m, lw_high, lw_low, new, new_high, new_low, x2, tops)
    return as_matrix(out.reshape(1024, 8, 128))


def local(matrix, pivot_rows, inv_lower, inv_upper):
    moved = pivot_rows >= TILE
    owner = jnp.where(moved, pivot_rows // TILE % 16, -1)
    index = jnp.arange(TILE, dtype=jnp.int32)
    before = (owner[:, None] == owner[None, :]) & (index[None, :] < index[:, None])
    rank = jnp.sum(before.astype(jnp.int32), axis=1)
    crowded = jnp.max(jnp.where(moved, rank, 0)) >= CAP
    out = few_pivots(matrix, pivot_rows, inv_lower, inv_upper, owner, rank)

    def body(state):
        return jnp.bool_(False), any_pivots(matrix, pivot_rows, inv_lower, inv_upper)

    return lax.while_loop(lambda state: state[0], body, (crowded, out))[1]


def solution(mesh):
    return jax.shard_map(
        local,
        mesh=mesh,
        in_specs=(P(None, "row", None, "col"), P(), P(), P()),
        out_specs=P(None, "row", None, "col"),
        check_vma=False,
    )
```

```python
import functools

import jax
import jax.numpy as jnp
from jax import lax
from jax.experimental import pallas as pl
from jax.experimental.pallas import tpu as pltpu
from jax.sharding import PartitionSpec as P

CAP = 48
TILE = 512
LAYERS = 8
MIB = 1024 * 1024
VMEM = 60 * MIB
STAY = 24
SHARE = 2 * CAP + STAY
ORDER = (4, 3, 5, 2, 6, 1, 7)


def spread(block, axis, holder):
    block = jnp.where(lax.axis_index(axis) == holder, block, jnp.zeros_like(block))
    return lax.psum(block, axis)


def any_pivots(matrix, pivot_rows, inv_lower, inv_upper):
    best = lax.Precision.HIGHEST
    tiles_down, tile_width, tiles_across, _ = matrix.shape
    row_count = lax.axis_size("row")
    row_index = lax.axis_index("row")
    col_index = lax.axis_index("col")
    local_rows = tiles_down * tile_width
    matrix_here = matrix.reshape(local_rows, tiles_across * tile_width)
    positions = jnp.arange(local_rows, dtype=jnp.int32)
    global_rows = (
        positions // tile_width * row_count + row_index
    ) * tile_width + positions % tile_width
    pivot_tile = pivot_rows // tile_width
    owned = pivot_tile % row_count == row_index
    pivot_local = pivot_tile // row_count * tile_width + pivot_rows % tile_width
    picked = jnp.where(
        owned[:, None], matrix_here[jnp.where(owned, pivot_local, 0)], jnp.float32(0.0)
    )
    former_top = spread(matrix_here[:tile_width], "row", 0)
    matches = (global_rows[:, None] == pivot_rows[None, :]) & (global_rows[:, None] >= tile_width)
    has_source = jnp.any(matches, axis=1)
    source = jnp.sum(
        jnp.where(matches, jnp.arange(tile_width, dtype=jnp.int32)[None, :], 0), axis=1
    )
    swapped = jnp.where(has_source[:, None], former_top[source], matrix_here)
    new_top = lax.psum(picked, "row")
    upper_rows = jnp.dot(inv_lower, new_top, precision=best, preferred_element_type=jnp.float32)
    panel_rows = swapped[:, :tile_width]
    solved_panel = jnp.dot(
        panel_rows, inv_upper, precision=best, preferred_element_type=jnp.float32
    )
    lower_cols = spread(solved_panel, "col", 0)
    updated = swapped - jnp.dot(
        lower_cols, upper_rows, precision=best, preferred_element_type=jnp.float32
    )
    leading = jnp.where(col_index == 0, lower_cols, updated[:, :tile_width])
    result = jnp.concatenate([leading, updated[:, tile_width:]], axis=1)
    first_rows = jnp.where(row_index == 0, upper_rows, result[:tile_width])
    result = jnp.concatenate([first_rows, result[tile_width:]], axis=0)
    return result.reshape(tiles_down, tile_width, tiles_across, tile_width)


def as_rows(matrix):
    return matrix.reshape(1024, 2, 4, 128).transpose(0, 2, 1, 3).reshape(1024, 8, 128)


def as_matrix(rows):
    return rows.reshape(1024, 4, 2, 128).transpose(0, 2, 1, 3).reshape(2, 512, 2, 512)


def split(value):
    high = value.astype(jnp.bfloat16)
    low = (value - high.astype(jnp.float32)).astype(jnp.bfloat16)
    return high, low


def dot3(a_high, a_low, b_high, b_low):
    dot = functools.partial(jnp.dot, preferred_element_type=jnp.float32)
    return dot(a_high, b_high) + (dot(a_high, b_low) + dot(a_low, b_high))


def whole(memory, count):
    return [pl.BlockSpec(memory_space=memory)] * count


def prepare_kernel(rows_ref, x_ref, first_ref, second_ref, picked_ref, *rest):
    outs, trades, (x_here, load) = rest[:LAYERS], rest[LAYERS : 2 * LAYERS + 1], rest[2 * LAYERS + 1 :]
    loads = [
        pltpu.make_async_copy(x_ref.at[pl.ds(2048 * b, 2048)], x_here.at[pl.ds(2048 * b, 2048)], load.at[b])
        for b in range(4)
    ]
    for copy in loads:
        copy.start()
    for b in range(4):
        loads[b].wait()
        out_ref = (first_ref, second_ref)[b // 2]
        for l in range(4):
            out_ref[256 * (b % 2) : 256 * (b % 2) + 256, 128 * l : 128 * l + 128] = x_here[
                pl.ds(2048 * b + 2 * l, 256, stride=8), :
            ]

    def row_of(at):
        return x_here[pl.ds(pl.multiple_of(rows_ref[at] * 8, 8), 8), :]

    @pl.loop(0, CAP)
    def _(k):
        picked_ref[pl.ds(pl.multiple_of(k * 8, 8), 8), :] = row_of(8 + k)

    @pl.when(rows_ref[1] == 0)
    def _():
        for k, out in enumerate(outs):
            for j in range(STAY):
                out[8 * j : 8 * j + 8, :] = row_of(8 + CAP + STAY * k + j)
        for k in range(16):
            out, at = (trades[LAYERS], 8 * CAP * (k // 2)) if k % 2 else (trades[k // 2], 0)

            @pl.loop(0, CAP, unroll=8)
            def _(j):
                out[pl.ds(pl.multiple_of(at + 8 * j, 8), 8), :] = row_of(8 + CAP + LAYERS * STAY + CAP * k + j)


def prepare(rows, x):
    half = jax.ShapeDtypeStruct((512, 512), jnp.float32)
    picked = jax.ShapeDtypeStruct((CAP * 8, 128), jnp.float32)
    piece = jax.ShapeDtypeStruct((STAY * 8, 128), jnp.float32)
    group = jax.ShapeDtypeStruct((8 * CAP * LAYERS, 128), jnp.float32)
    return pl.pallas_call(
        prepare_kernel,
        out_shape=[half, half, picked] + [piece] * LAYERS + [picked] * LAYERS + [group],
        in_specs=whole(pltpu.SMEM, 1) + whole(pl.ANY, 1),
        out_specs=whole(pltpu.VMEM, 2 * LAYERS + 4),
        scratch_shapes=[pltpu.VMEM((8192, 128), jnp.float32), pltpu.SemaphoreType.DMA((4,))],
        compiler_params=pltpu.CompilerParams(vmem_limit_bytes=20 * MIB),
        cost_estimate=pl.CostEstimate(flops=0, bytes_accessed=10 * MIB, transcendentals=0),
        name="prepare",
    )(rows, x)


def solve_kernel(rows_ref, half_ref, other_ref, sent_ref, inv_ref, high_ref, low_ref, swapped):
    core, x = rows_ref[2] % 2, rows_ref[2] // 2 % 4
    for ref, tile in ((half_ref, core), (other_ref, 1 - core)):
        for at, size, ahead, skip in ((0, 128, 0, 0), (128, 128, 3, 0), (256, 128, 1, 0), (384, 64, 2, 0), (448, 64, 2, 64)):
            to = tile * 512 + lax.rem(x + ahead, 4) * 128 + skip
            swapped[pl.ds(pl.multiple_of(to, 64), size), :] = ref[at : at + size, :]

    @pl.loop(0, rows_ref[0])
    def _(k):
        swapped[pl.ds(rows_ref[8 + k], 1), :] = sent_ref[pl.ds(k, 1), :]

    inv_high, inv_low = split(inv_ref[...])

    @pl.loop(0, 4)
    def _(b):
        at = pl.ds(pl.multiple_of(b * 256, 256), 256)
        high, low = split(swapped[at, :])
        high_ref[at, :], low_ref[at, :] = split(dot3(high, low, inv_high, inv_low))


def solve(rows, half, other, sent, inv_upper):
    part = jax.ShapeDtypeStruct((1024, 512), jnp.bfloat16)
    return pl.pallas_call(
        solve_kernel,
        out_shape=[part, part],
        in_specs=whole(pltpu.SMEM, 1) + whole(pltpu.VMEM, 4),
        out_specs=whole(pltpu.VMEM, 2),
        scratch_shapes=[pltpu.VMEM((1024, 512), jnp.float32)],
        compiler_params=pltpu.CompilerParams(vmem_limit_bytes=VMEM),
        cost_estimate=pl.CostEstimate(flops=3 * 2 * 1024 * 512 * 512, bytes_accessed=6 * MIB, transcendentals=0),
        name="solve",
    )(rows, half, other, sent, inv_upper)


def spread_rows(ref, g_high, g_low):
    count = ref.shape[0] // 8
    for sub in range(8):
        high, low = split(ref[pl.ds(sub, count, stride=8), :])
        g_high[:, 128 * sub : 128 * sub + 128] = high
        g_low[:, 128 * sub : 128 * sub + 128] = low


def trailing_kernel(
    rows_ref, x_ref, gathered_all, l_high_all, l_low_all, w_all, new_ref, out_ref,
    gathered, new_top, l_high, l_low, w_ref, g_high, g_low, u_high, u_low, load,
):
    step = pl.program_id(0)

    @pl.when(step == 0)
    def _():
        moves = ((gathered_all, gathered), (w_all, w_ref), (l_high_all, l_high), (l_low_all, l_low))
        copies = [pltpu.make_async_copy(ref, to, load.at[k]) for k, (ref, to) in enumerate(moves)]
        for copy in copies:
            copy.start()
        copies[0].wait()

        @pl.loop(0, TILE, unroll=8)
        def _(k):
            at = pl.ds(pl.multiple_of(rows_ref[8 + CAP + k] * 8, 8), 8)
            new_top[pl.ds(pl.multiple_of(k * 8, 8), 8), :] = gathered[at, :]

        spread_rows(new_top, g_high, g_low)
        copies[1].wait()
        w_high, w_low = split(w_ref[...])
        for n in range(4):
            at = slice(256 * n, 256 * n + 256)
            u_high[:, at], u_low[:, at] = split(dot3(w_high, w_low, g_high[:, at], g_low[:, at]))
        copies[2].wait()
        copies[3].wait()

    @pl.when(step > 0)
    def _():
        block = step - 1
        out_ref[...] = x_ref[...]

        @pl.loop(rows_ref[2 + step], rows_ref[3 + step])
        def _(k):
            to = pl.ds(pl.multiple_of((rows_ref[8 + k] - block * 256) * 8, 8), 8)
            out_ref[to, :] = new_ref[pl.ds(pl.multiple_of(k * 8, 8), 8), :]

        here = pl.ds(pl.multiple_of(block * 256, 256), 256)
        high, low = l_high[here, :], l_low[here, :]
        for n in range(4):
            at = slice(256 * n, 256 * n + 256)
            product = dot3(high, low, u_high[:, at], u_low[:, at])
            for part in range(2):
                to = pl.ds(2 * n + part, 256, stride=8)
                out_ref[to, :] = out_ref[to, :] - product[:, 128 * part : 128 * part + 128]

        @pl.when(rows_ref[2] == 0)
        def _():
            lower = high.astype(jnp.float32) + low.astype(jnp.float32)
            for l in range(4):
                out_ref[pl.ds(2 * l, 256, stride=8), :] = lower[:, 128 * l : 128 * l + 128]

        @pl.when((rows_ref[1] == 0) & (block < 2))
        def _():
            at = pl.ds(pl.multiple_of(lax.rem(block, 2) * 256, 256), 256)
            for sub in range(8):
                cols = slice(128 * sub, 128 * sub + 128)
                u = u_high[at, cols].astype(jnp.float32) + u_low[at, cols].astype(jnp.float32)
                out_ref[pl.ds(sub, 256, stride=8), :] = u


def trailing(rows, x, gathered, l_high, l_low, weights, new):
    block = pl.BlockSpec((2048, 128), lambda i, *_: (jnp.maximum(i - 1, 0), 0))
    return pl.pallas_call(
        trailing_kernel,
        out_shape=jax.ShapeDtypeStruct((8192, 128), jnp.float32),
        grid_spec=pltpu.PrefetchScalarGridSpec(
            num_scalar_prefetch=1,
            grid=(5,),
            in_specs=[block] + whole(pl.ANY, 4) + whole(pltpu.VMEM, 1),
            out_specs=block,
            scratch_shapes=[pltpu.VMEM((8 * LAYERS * SHARE, 128), jnp.float32), pltpu.VMEM((4096, 128), jnp.float32)]
            + [pltpu.VMEM((1024, 512), jnp.bfloat16)] * 2
            + [pltpu.VMEM((512, 512), jnp.float32)]
            + [pltpu.VMEM((512, 1024), jnp.bfloat16)] * 4
            + [pltpu.SemaphoreType.DMA((4,))],
        ),
        compiler_params=pltpu.CompilerParams(vmem_limit_bytes=VMEM),
        cost_estimate=pl.CostEstimate(flops=3 * 2 * 1024 * 512 * 1536, bytes_accessed=18 * MIB, transcendentals=0),
        name="trailing",
    )(rows, x, gathered, l_high, l_low, weights, new)


def x_shift(value, by):
    return lax.ppermute(value, "col", [(i, i // 8 * 8 + (i // 2 + by) % 4 * 2 + i % 2) for i in range(16)])


def swap(value, axis):
    return lax.ppermute(value, axis, [(i, i ^ 1) for i in range(16)])


def gather_layers(piece):
    groups = [[2 * i + j for i in range(LAYERS)] for j in range(2)]
    return lax.all_gather(piece, "row", axis_index_groups=groups, axis=0, tiled=True)


def scatter_panel(first, second, col):
    core, x = col % 2, col // 2 % 4
    half = jnp.where(core == 0, first, lax.ppermute(second, "col", [(0, 1)]))
    mine = jnp.where(x == 0, half[:128], 0.0)
    got = [
        lax.ppermute(half[128 * to : 128 * to + 128], "col", [(0, 2 * to), (1, 2 * to + 1)])
        for to in (1, 3, 2)
    ]
    return jnp.where(col < 8, mine + got[0] + got[1] + got[2], 0.0)


def gather_panel(mine):
    mine = mine + lax.ppermute(mine, "col", [(i, i + 8) for i in range(8)])
    up, down = x_shift(mine, 1), x_shift(mine, -1)
    half = jnp.concatenate([mine, up, down, x_shift(up[:64], 1), x_shift(down[64:], -1)])
    return half, swap(half, "col")


def across(value, col):
    value = jnp.where(col == 0, value, 0.0)
    value = value + lax.ppermute(value, "col", [(0, 1)])
    got = [lax.ppermute(value, "col", [(0, 2 * to), (1, 2 * to + 1)]) for to in (1, 3, 2)]
    value = value + got[0] + got[1] + got[2]
    return value + lax.ppermute(value, "col", [(i, i + 8) for i in range(8)])


def few_pivots(matrix, pivot_rows, inv_lower, inv_upper, owner, rank):
    row, col = lax.axis_index("row"), lax.axis_index("col")
    y = row % 2
    x2 = as_rows(matrix).reshape(8192, 128)

    index = jnp.arange(TILE, dtype=jnp.int32)
    here = pivot_rows // TILE // 16 * TILE + pivot_rows % TILE
    capped = jnp.minimum(rank, jnp.where(owner < 0, LAYERS * STAY, CAP) - 1)
    key = jnp.where(owner < 0, -1, owner * CAP + capped)

    def listed(keys, values, count, first=0):
        slots = jnp.arange(count, dtype=jnp.int32) + first
        return jnp.sum(jnp.where(keys[:, None] == slots[None, :], values[:, None], 0), axis=0)

    at_rows = jnp.minimum(listed(key - row * CAP, here, CAP), 1023)
    staying = jnp.minimum(listed(jnp.where(owner < 0, capped, -1), index, LAYERS * STAY), TILE - 1)
    going = jnp.minimum(listed(key, index, 16 * CAP), TILE - 1)
    moved_at = owner // 2 * SHARE + owner % 2 * CAP + capped
    stay_at = capped // STAY * SHARE + 2 * CAP + capped % STAY
    lies_at = jnp.where(owner < 0, stay_at, moved_at)
    limits = 256 * jnp.arange(5, dtype=jnp.int32)
    below = jnp.sum(((owner == row)[None] & (here[None] < limits[:, None])).astype(jnp.int32), axis=1)
    below = jnp.minimum(below, CAP)
    place = jnp.stack([row, col]).astype(jnp.int32)
    rows = jnp.concatenate([below[4:], place, below, at_rows, lies_at])
    head = jnp.concatenate([jnp.zeros(1, jnp.int32), place, jnp.zeros(5, jnp.int32)])
    first, second, picked, *sends = prepare(jnp.concatenate([head, at_rows, staying, going]), x2)
    share, packed = sends[:LAYERS], sends[LAYERS:]

    odd = lax.ppermute(packed[LAYERS], "row", [(0, 1)])
    pieces = [jnp.where(row == 0, packed[k], odd[8 * CAP * k : 8 * CAP * (k + 1)]) for k in range(LAYERS)]
    new = jnp.where(row < 2, pieces[0], 0.0)
    for to in ORDER:
        new = new + lax.ppermute(pieces[to], "row", [(0, 2 * to), (1, 2 * to + 1)])

    paired = swap(picked, "row")
    piece = jnp.where(row == 0, share[0], 0.0)
    for to in ORDER:
        piece = piece + lax.ppermute(share[to], "row", [(0, 2 * to)])
    piece = piece + lax.ppermute(piece, "row", [(2 * i, 2 * i + 1) for i in range(LAYERS)])
    gathered = gather_layers(
        jnp.concatenate([jnp.where(y == 0, picked, paired), jnp.where(y == 0, paired, picked), piece])
    )

    half, other_half = gather_panel(scatter_panel(first, second, col))
    sent = across(new.reshape(CAP, 4, 2, 128)[:, :, 0].reshape(CAP, TILE), col)
    l_high, l_low = solve(rows, half, other_half, sent, inv_upper)
    out = trailing(rows, x2, gathered, l_high, l_low, inv_lower, new)
    return as_matrix(out.reshape(1024, 8, 128))


def local(matrix, pivot_rows, inv_lower, inv_upper):
    moved = pivot_rows >= TILE
    owner = jnp.where(moved, pivot_rows // TILE % 16, -1)
    before = (owner[:, None] == owner[None, :]) & (pivot_rows[None, :] < pivot_rows[:, None])
    rank = jnp.sum(before.astype(jnp.int32), axis=1)
    crowded = jnp.any(rank >= jnp.where(moved, CAP, LAYERS * STAY))
    out = few_pivots(matrix, pivot_rows, inv_lower, inv_upper, owner, rank)

    def body(state):
        return jnp.bool_(False), any_pivots(matrix, pivot_rows, inv_lower, inv_upper)

    return lax.while_loop(lambda state: state[0], body, (crowded, out))[1]


def solution(mesh):
    return jax.shard_map(
        local,
        mesh=mesh,
        in_specs=(P(None, "row", None, "col"), P(), P(), P()),
        out_specs=P(None, "row", None, "col"),
        check_vma=False,
    )
```

```python
import functools

import jax
import jax.numpy as jnp
from jax import lax
from jax.experimental import pallas as pl
from jax.experimental.pallas import tpu as pltpu
from jax.sharding import PartitionSpec as P

CAP = 48
TILE = 512
LAYERS = 8
MIB = 1024 * 1024
VMEM = 60 * MIB
STAY = 24
SHARE = 2 * CAP + STAY
ORDER = (4, 3, 5, 2, 6, 1, 7)


def spread(block, axis, holder):
    block = jnp.where(lax.axis_index(axis) == holder, block, jnp.zeros_like(block))
    return lax.psum(block, axis)


def any_pivots(matrix, pivot_rows, inv_lower, inv_upper):
    best = lax.Precision.HIGHEST
    tiles_down, tile_width, tiles_across, _ = matrix.shape
    row_count = lax.axis_size("row")
    row_index = lax.axis_index("row")
    col_index = lax.axis_index("col")
    local_rows = tiles_down * tile_width
    matrix_here = matrix.reshape(local_rows, tiles_across * tile_width)
    positions = jnp.arange(local_rows, dtype=jnp.int32)
    global_rows = (
        positions // tile_width * row_count + row_index
    ) * tile_width + positions % tile_width
    pivot_tile = pivot_rows // tile_width
    owned = pivot_tile % row_count == row_index
    pivot_local = pivot_tile // row_count * tile_width + pivot_rows % tile_width
    picked = jnp.where(
        owned[:, None], matrix_here[jnp.where(owned, pivot_local, 0)], jnp.float32(0.0)
    )
    former_top = spread(matrix_here[:tile_width], "row", 0)
    matches = (global_rows[:, None] == pivot_rows[None, :]) & (global_rows[:, None] >= tile_width)
    has_source = jnp.any(matches, axis=1)
    source = jnp.sum(
        jnp.where(matches, jnp.arange(tile_width, dtype=jnp.int32)[None, :], 0), axis=1
    )
    swapped = jnp.where(has_source[:, None], former_top[source], matrix_here)
    new_top = lax.psum(picked, "row")
    upper_rows = jnp.dot(inv_lower, new_top, precision=best, preferred_element_type=jnp.float32)
    panel_rows = swapped[:, :tile_width]
    solved_panel = jnp.dot(
        panel_rows, inv_upper, precision=best, preferred_element_type=jnp.float32
    )
    lower_cols = spread(solved_panel, "col", 0)
    updated = swapped - jnp.dot(
        lower_cols, upper_rows, precision=best, preferred_element_type=jnp.float32
    )
    leading = jnp.where(col_index == 0, lower_cols, updated[:, :tile_width])
    result = jnp.concatenate([leading, updated[:, tile_width:]], axis=1)
    first_rows = jnp.where(row_index == 0, upper_rows, result[:tile_width])
    result = jnp.concatenate([first_rows, result[tile_width:]], axis=0)
    return result.reshape(tiles_down, tile_width, tiles_across, tile_width)


def as_rows(matrix):
    return matrix.reshape(1024, 2, 4, 128).transpose(0, 2, 1, 3).reshape(1024, 8, 128)


def as_matrix(rows):
    return rows.reshape(1024, 4, 2, 128).transpose(0, 2, 1, 3).reshape(2, 512, 2, 512)


def split(value):
    high = value.astype(jnp.bfloat16)
    low = (value - high.astype(jnp.float32)).astype(jnp.bfloat16)
    return high, low


def dot3(a_high, a_low, b_high, b_low):
    dot = functools.partial(jnp.dot, preferred_element_type=jnp.float32)
    return dot(a_high, b_high) + (dot(a_high, b_low) + dot(a_low, b_high))


def whole(memory, count):
    return [pl.BlockSpec(memory_space=memory)] * count


def prepare_kernel(rows_ref, x_ref, first_ref, second_ref, picked_ref, *rest):
    outs, (x_here, load) = rest[:LAYERS], rest[LAYERS:]
    loads = [
        pltpu.make_async_copy(x_ref.at[pl.ds(2048 * b, 2048)], x_here.at[pl.ds(2048 * b, 2048)], load.at[b])
        for b in range(4)
    ]
    for copy in loads:
        copy.start()
    for b in range(4):
        loads[b].wait()
        out_ref = (first_ref, second_ref)[b // 2]
        for l in range(4):
            out_ref[256 * (b % 2) : 256 * (b % 2) + 256, 128 * l : 128 * l + 128] = x_here[
                pl.ds(2048 * b + 2 * l, 256, stride=8), :
            ]

    def row_of(at):
        return x_here[pl.ds(pl.multiple_of(rows_ref[at] * 8, 8), 8), :]

    @pl.loop(0, CAP)
    def _(k):
        picked_ref[pl.ds(pl.multiple_of(k * 8, 8), 8), :] = row_of(8 + k)

    @pl.when(rows_ref[1] == 0)
    def _():
        for k, out in enumerate(outs):
            for j in range(STAY):
                out[8 * j : 8 * j + 8, :] = row_of(8 + CAP + STAY * k + j)


def prepare(rows, x):
    half = jax.ShapeDtypeStruct((512, 512), jnp.float32)
    picked = jax.ShapeDtypeStruct((CAP * 8, 128), jnp.float32)
    piece = jax.ShapeDtypeStruct((STAY * 8, 128), jnp.float32)
    return pl.pallas_call(
        prepare_kernel,
        out_shape=[half, half, picked] + [piece] * LAYERS,
        in_specs=whole(pltpu.SMEM, 1) + whole(pl.ANY, 1),
        out_specs=whole(pltpu.VMEM, LAYERS + 3),
        scratch_shapes=[pltpu.VMEM((8192, 128), jnp.float32), pltpu.SemaphoreType.DMA((4,))],
        compiler_params=pltpu.CompilerParams(vmem_limit_bytes=20 * MIB),
        cost_estimate=pl.CostEstimate(flops=0, bytes_accessed=10 * MIB, transcendentals=0),
        name="prepare",
    )(rows, x)


def pack_kernel(rows_ref, x_ref, *rest):
    outs, (x_here, load) = rest[: LAYERS + 1], rest[LAYERS + 1 :]

    @pl.when(rows_ref[0] == 0)
    def _():
        copy = pltpu.make_async_copy(x_ref.at[pl.ds(0, 4096)], x_here, load)
        copy.start()
        copy.wait()
        places = [(outs[LAYERS], 8 * CAP * (k // 2)) if k % 2 else (outs[k // 2], 0) for k in range(16)]
        for k, (out, at) in enumerate(places):

            @pl.loop(0, CAP, unroll=8)
            def _(j):
                to = pl.ds(pl.multiple_of(at + 8 * j, 8), 8)
                out[to, :] = x_here[pl.ds(pl.multiple_of(rows_ref[8 + CAP * k + j] * 8, 8), 8), :]


def pack(rows, x):
    piece = jax.ShapeDtypeStruct((8 * CAP, 128), jnp.float32)
    group = jax.ShapeDtypeStruct((8 * CAP * LAYERS, 128), jnp.float32)
    return pl.pallas_call(
        pack_kernel,
        out_shape=[piece] * LAYERS + [group],
        in_specs=whole(pltpu.SMEM, 1) + whole(pl.ANY, 1),
        out_specs=whole(pltpu.VMEM, LAYERS + 1),
        scratch_shapes=[pltpu.VMEM((4096, 128), jnp.float32), pltpu.SemaphoreType.DMA(())],
        compiler_params=pltpu.CompilerParams(vmem_limit_bytes=20 * MIB),
        cost_estimate=pl.CostEstimate(flops=0, bytes_accessed=6 * MIB, transcendentals=0),
        name="pack",
    )(rows, x)


def solve_kernel(rows_ref, half_ref, other_ref, sent_ref, inv_ref, high_ref, low_ref, swapped):
    core, x = rows_ref[2] % 2, rows_ref[2] // 2 % 4
    for ref, tile in ((half_ref, core), (other_ref, 1 - core)):
        for at, size, ahead, skip in ((0, 128, 0, 0), (128, 128, 3, 0), (256, 128, 1, 0), (384, 64, 2, 0), (448, 64, 2, 64)):
            to = tile * 512 + lax.rem(x + ahead, 4) * 128 + skip
            swapped[pl.ds(pl.multiple_of(to, 64), size), :] = ref[at : at + size, :]

    @pl.loop(0, rows_ref[0])
    def _(k):
        swapped[pl.ds(rows_ref[8 + k], 1), :] = sent_ref[pl.ds(k, 1), :]

    inv_high, inv_low = split(inv_ref[...])

    @pl.loop(0, 4)
    def _(b):
        at = pl.ds(pl.multiple_of(b * 256, 256), 256)
        high, low = split(swapped[at, :])
        high_ref[at, :], low_ref[at, :] = split(dot3(high, low, inv_high, inv_low))


def solve(rows, half, other, sent, inv_upper):
    part = jax.ShapeDtypeStruct((1024, 512), jnp.bfloat16)
    return pl.pallas_call(
        solve_kernel,
        out_shape=[part, part],
        in_specs=whole(pltpu.SMEM, 1) + whole(pltpu.VMEM, 4),
        out_specs=whole(pltpu.VMEM, 2),
        scratch_shapes=[pltpu.VMEM((1024, 512), jnp.float32)],
        compiler_params=pltpu.CompilerParams(vmem_limit_bytes=VMEM),
        cost_estimate=pl.CostEstimate(flops=3 * 2 * 1024 * 512 * 512, bytes_accessed=6 * MIB, transcendentals=0),
        name="solve",
    )(rows, half, other, sent, inv_upper)


def spread_rows(ref, g_high, g_low):
    count = ref.shape[0] // 8
    for sub in range(8):
        high, low = split(ref[pl.ds(sub, count, stride=8), :])
        g_high[:, 128 * sub : 128 * sub + 128] = high
        g_low[:, 128 * sub : 128 * sub + 128] = low


def trailing_kernel(
    rows_ref, x_ref, gathered_all, l_high_all, l_low_all, w_all, new_ref, out_ref,
    gathered, new_top, l_high, l_low, w_ref, g_high, g_low, u_high, u_low, load,
):
    step = pl.program_id(0)

    @pl.when(step == 0)
    def _():
        moves = ((gathered_all, gathered), (w_all, w_ref), (l_high_all, l_high), (l_low_all, l_low))
        copies = [pltpu.make_async_copy(ref, to, load.at[k]) for k, (ref, to) in enumerate(moves)]
        for copy in copies:
            copy.start()
        copies[0].wait()

        @pl.loop(0, TILE, unroll=8)
        def _(k):
            at = pl.ds(pl.multiple_of(rows_ref[8 + CAP + k] * 8, 8), 8)
            new_top[pl.ds(pl.multiple_of(k * 8, 8), 8), :] = gathered[at, :]

        spread_rows(new_top, g_high, g_low)
        copies[1].wait()
        w_high, w_low = split(w_ref[...])
        for n in range(4):
            at = slice(256 * n, 256 * n + 256)
            u_high[:, at], u_low[:, at] = split(dot3(w_high, w_low, g_high[:, at], g_low[:, at]))
        copies[2].wait()
        copies[3].wait()

    @pl.when(step > 0)
    def _():
        block = step - 1
        out_ref[...] = x_ref[...]

        @pl.loop(rows_ref[2 + step], rows_ref[3 + step])
        def _(k):
            to = pl.ds(pl.multiple_of((rows_ref[8 + k] - block * 256) * 8, 8), 8)
            out_ref[to, :] = new_ref[pl.ds(pl.multiple_of(k * 8, 8), 8), :]

        here = pl.ds(pl.multiple_of(block * 256, 256), 256)
        high, low = l_high[here, :], l_low[here, :]
        for n in range(4):
            at = slice(256 * n, 256 * n + 256)
            product = dot3(high, low, u_high[:, at], u_low[:, at])
            for part in range(2):
                to = pl.ds(2 * n + part, 256, stride=8)
                out_ref[to, :] = out_ref[to, :] - product[:, 128 * part : 128 * part + 128]

        @pl.when(rows_ref[2] == 0)
        def _():
            lower = high.astype(jnp.float32) + low.astype(jnp.float32)
            for l in range(4):
                out_ref[pl.ds(2 * l, 256, stride=8), :] = lower[:, 128 * l : 128 * l + 128]

        @pl.when((rows_ref[1] == 0) & (block < 2))
        def _():
            at = pl.ds(pl.multiple_of(lax.rem(block, 2) * 256, 256), 256)
            for sub in range(8):
                cols = slice(128 * sub, 128 * sub + 128)
                u = u_high[at, cols].astype(jnp.float32) + u_low[at, cols].astype(jnp.float32)
                out_ref[pl.ds(sub, 256, stride=8), :] = u


def trailing(rows, x, gathered, l_high, l_low, weights, new):
    block = pl.BlockSpec((2048, 128), lambda i, *_: (jnp.maximum(i - 1, 0), 0))
    return pl.pallas_call(
        trailing_kernel,
        out_shape=jax.ShapeDtypeStruct((8192, 128), jnp.float32),
        grid_spec=pltpu.PrefetchScalarGridSpec(
            num_scalar_prefetch=1,
            grid=(5,),
            in_specs=[block] + whole(pl.ANY, 4) + whole(pltpu.VMEM, 1),
            out_specs=block,
            scratch_shapes=[pltpu.VMEM((8 * LAYERS * SHARE, 128), jnp.float32), pltpu.VMEM((4096, 128), jnp.float32)]
            + [pltpu.VMEM((1024, 512), jnp.bfloat16)] * 2
            + [pltpu.VMEM((512, 512), jnp.float32)]
            + [pltpu.VMEM((512, 1024), jnp.bfloat16)] * 4
            + [pltpu.SemaphoreType.DMA((4,))],
        ),
        compiler_params=pltpu.CompilerParams(vmem_limit_bytes=VMEM),
        cost_estimate=pl.CostEstimate(flops=3 * 2 * 1024 * 512 * 1536, bytes_accessed=18 * MIB, transcendentals=0),
        name="trailing",
    )(rows, x, gathered, l_high, l_low, weights, new)


def x_shift(value, by):
    return lax.ppermute(value, "col", [(i, i // 8 * 8 + (i // 2 + by) % 4 * 2 + i % 2) for i in range(16)])


def swap(value, axis):
    return lax.ppermute(value, axis, [(i, i ^ 1) for i in range(16)])


def gather_layers(piece):
    groups = [[2 * i + j for i in range(LAYERS)] for j in range(2)]
    return lax.all_gather(piece, "row", axis_index_groups=groups, axis=0, tiled=True)


def scatter_panel(first, second, col):
    core, x = col % 2, col // 2 % 4
    half = jnp.where(core == 0, first, lax.ppermute(second, "col", [(0, 1)]))
    mine = jnp.where(x == 0, half[:128], 0.0)
    got = [
        lax.ppermute(half[128 * to : 128 * to + 128], "col", [(0, 2 * to), (1, 2 * to + 1)])
        for to in (1, 3, 2)
    ]
    return jnp.where(col < 8, mine + got[0] + got[1] + got[2], 0.0)


def gather_panel(mine):
    mine = mine + lax.ppermute(mine, "col", [(i, i + 8) for i in range(8)])
    up, down = x_shift(mine, 1), x_shift(mine, -1)
    half = jnp.concatenate([mine, up, down, x_shift(up[:64], 1), x_shift(down[64:], -1)])
    return half, swap(half, "col")


def across(value, col):
    value = jnp.where(col == 0, value, 0.0)
    value = value + lax.ppermute(value, "col", [(0, 1)])
    got = [lax.ppermute(value, "col", [(0, 2 * to), (1, 2 * to + 1)]) for to in (1, 3, 2)]
    value = value + got[0] + got[1] + got[2]
    return value + lax.ppermute(value, "col", [(i, i + 8) for i in range(8)])


def few_pivots(matrix, pivot_rows, inv_lower, inv_upper, owner, rank):
    row, col = lax.axis_index("row"), lax.axis_index("col")
    y = row % 2
    x2 = as_rows(matrix).reshape(8192, 128)

    index = jnp.arange(TILE, dtype=jnp.int32)
    here = pivot_rows // TILE // 16 * TILE + pivot_rows % TILE
    capped = jnp.minimum(rank, jnp.where(owner < 0, LAYERS * STAY, CAP) - 1)
    key = jnp.where(owner < 0, -1, owner * CAP + capped)

    def listed(keys, values, count, first=0):
        slots = jnp.arange(count, dtype=jnp.int32) + first
        return jnp.sum(jnp.where(keys[:, None] == slots[None, :], values[:, None], 0), axis=0)

    at_rows = jnp.minimum(listed(key - row * CAP, here, CAP), 1023)
    staying = jnp.minimum(listed(jnp.where(owner < 0, capped, -1), index, LAYERS * STAY), TILE - 1)
    going = jnp.minimum(listed(key, index, 16 * CAP), TILE - 1)
    moved_at = owner // 2 * SHARE + owner % 2 * CAP + capped
    stay_at = capped // STAY * SHARE + 2 * CAP + capped % STAY
    lies_at = jnp.where(owner < 0, stay_at, moved_at)
    limits = 256 * jnp.arange(5, dtype=jnp.int32)
    below = jnp.sum(((owner == row)[None] & (here[None] < limits[:, None])).astype(jnp.int32), axis=1)
    below = jnp.minimum(below, CAP)
    place = jnp.stack([row, col]).astype(jnp.int32)
    rows = jnp.concatenate([below[4:], place, below, at_rows, lies_at])
    head = jnp.concatenate([jnp.zeros(1, jnp.int32), place, jnp.zeros(5, jnp.int32)])
    first, second, picked, *share = prepare(jnp.concatenate([head, at_rows, staying]), x2)

    packed = pack(jnp.concatenate([row[None].astype(jnp.int32), jnp.zeros(7, jnp.int32), going]), x2)
    odd = lax.ppermute(packed[LAYERS], "row", [(0, 1)])
    pieces = [jnp.where(row == 0, packed[k], odd[8 * CAP * k : 8 * CAP * (k + 1)]) for k in range(LAYERS)]
    new = jnp.where(row < 2, pieces[0], 0.0)
    for to in ORDER:
        new = new + lax.ppermute(pieces[to], "row", [(0, 2 * to), (1, 2 * to + 1)])

    paired = swap(picked, "row")
    piece = jnp.where(row == 0, share[0], 0.0)
    for to in ORDER:
        piece = piece + lax.ppermute(share[to], "row", [(0, 2 * to)])
    piece = piece + lax.ppermute(piece, "row", [(2 * i, 2 * i + 1) for i in range(LAYERS)])
    gathered = gather_layers(
        jnp.concatenate([jnp.where(y == 0, picked, paired), jnp.where(y == 0, paired, picked), piece])
    )

    half, other_half = gather_panel(scatter_panel(first, second, col))
    sent = across(new.reshape(CAP, 4, 2, 128)[:, :, 0].reshape(CAP, TILE), col)
    l_high, l_low = solve(rows, half, other_half, sent, inv_upper)
    out = trailing(rows, x2, gathered, l_high, l_low, inv_lower, new)
    return as_matrix(out.reshape(1024, 8, 128))


def local(matrix, pivot_rows, inv_lower, inv_upper):
    moved = pivot_rows >= TILE
    owner = jnp.where(moved, pivot_rows // TILE % 16, -1)
    before = (owner[:, None] == owner[None, :]) & (pivot_rows[None, :] < pivot_rows[:, None])
    rank = jnp.sum(before.astype(jnp.int32), axis=1)
    crowded = jnp.any(rank >= jnp.where(moved, CAP, LAYERS * STAY))
    out = few_pivots(matrix, pivot_rows, inv_lower, inv_upper, owner, rank)

    def body(state):
        return jnp.bool_(False), any_pivots(matrix, pivot_rows, inv_lower, inv_upper)

    return lax.while_loop(lambda state: state[0], body, (crowded, out))[1]


def solution(mesh):
    return jax.shard_map(
        local,
        mesh=mesh,
        in_specs=(P(None, "row", None, "col"), P(), P(), P()),
        out_specs=P(None, "row", None, "col"),
        check_vma=False,
    )
```
